32 devices in a mesh: wide: 8 (over z, y), narrow: 4 (over x, core).
Axes of the slice: x: 2, y: 2, z: 4, core: 2. Of those that a mesh axis runs over, the one named last changes fastest.
Arguments:
- embedding: float32 [16384, 128], P(('wide', 'narrow'))
- tile_blocks: bfloat16 [8, 4, 22, 512, 512], P('wide', 'narrow'), may hold values from -0.125 to 0.125
- tile_row: int32 [8, 4, 22], P('wide', 'narrow'), may hold values from 0 to 3
- tile_col: int32 [8, 4, 22], P('wide', 'narrow'), may hold values from 0 to 7
- counts: int32 [8, 4], P('wide', 'narrow'), may hold values from 1 to 22, as said below
Outputs:
- orthonormal: float32 [16384, 128], P(('wide', 'narrow'))
The draws below stay inside these ranges and needn't reach their ends.
Inputs may be any that keep to these rules, and one draw needn't show every extreme that they name: Slots 0 to counts[w, n] - 1 of device (w, n) hold its tiles, the others are unused; some device has all 22 slots live.
All inputs are finite; a program needn't handle non-finite values.
Results may differ from the reference program's by a relative error of at most 0.0036.
Values may be sent and summed in bfloat16 or wider, within the bound.
A program may use at most 64 MiB of HBM per device.

```python
import math
import jax
import jax.numpy as jnp
from jax import lax

TILE = 512
EMB = 128
TILE_ROWS = 1
SLOTS = 22
WIDE_DEVS = 8
NARROW_DEVS = 4
SLAB_TILES = 4
GROUP_TILES = 8
NODES = 16384
N_WIDE = 8
N_NARROW = 4


def draw_embedding(key, part):
    keys = jax.random.split(jax.random.fold_in(key, 11), 3)
    row_pos = jnp.arange(NODES, dtype=jnp.float32)[:, None] / NODES
    row_scale = jnp.exp(math.log(3.0) * row_pos) * jnp.exp(jax.random.uniform(keys[1], (NODES, 1), jnp.float32, -math.log(2.0), math.log(2.0)))
    col_scale = jnp.exp(jax.random.uniform(keys[2], (1, EMB), jnp.float32, 0.0, math.log(10.0)))
    base = jax.random.normal(keys[0], (NODES, EMB), jnp.float32)
    return base * row_scale * col_scale / 4.0


def draw_counts(key, part):
    keys = jax.random.split(jax.random.fold_in(key, 23), 2)
    drawn = jax.random.randint(keys[0], (WIDE_DEVS, NARROW_DEVS), 0, SLOTS, jnp.int32)
    filled = 1 + drawn * (drawn + SLOTS) // (2 * SLOTS)
    flat_counts = filled.reshape(-1)
    position = jax.random.randint(keys[1], (), 0, WIDE_DEVS * NARROW_DEVS, jnp.int32)
    flat_counts = flat_counts.at[position].set(SLOTS)
    return flat_counts.reshape(WIDE_DEVS, NARROW_DEVS).astype(jnp.int32)


def plant(array, own_key, smallest, largest):
    extent = array.shape
    place = [jax.random.randint(jax.random.fold_in(own_key, axis), (), 0, extent[axis]) for axis in range(len(extent))]
    array = array.at[tuple(place)].set(smallest)
    longest = extent.index(max(extent))
    place[longest] = (place[longest] + 1) % extent[longest]
    return array.at[tuple(place)].set(largest)


def level_of(rng, shape, cuts, least, largest):
    gain = 1.0
    for dim, shards_of in cuts:
        draws = jax.random.uniform(jax.random.fold_in(jax.random.fold_in(rng, 6), dim), (shards_of,), jnp.float32, least / len(cuts), largest / len(cuts))
        gain = gain * jnp.repeat(jnp.exp(draws), shape[dim] // shards_of).reshape((-1,) + (1,) * (len(shape) - 1 - dim))
    return gain


def normal_values(own_key, dims, deviation, bound, cuts=(), kind=jnp.bfloat16):
    gain = level_of(own_key, dims, cuts, -0.22, 0.18) if cuts else 1.0
    values = jax.random.normal(own_key, dims, jnp.float32) * deviation * gain
    return jnp.minimum(jnp.maximum(values, -bound), bound).astype(kind)


def setup_inputs(seed: int = 0) -> dict:
    key_of = jax.random.split(jax.random.key(seed), 6)
    embedding = draw_embedding(jax.random.fold_in(key_of[5], 71), 0)
    tile_blocks = normal_values(key_of[1], (WIDE_DEVS, NARROW_DEVS, SLOTS, TILE, TILE), (4 * TILE) ** -0.5, 0.125, ((0, 8), (1, 4)))
    tile_row = plant(jax.random.randint(key_of[2], (WIDE_DEVS, NARROW_DEVS, SLOTS), 0, SLAB_TILES), jax.random.fold_in(key_of[2], 1), 0, SLAB_TILES - 1).astype(jnp.int32)
    tile_col = plant(jax.random.randint(key_of[3], (WIDE_DEVS, NARROW_DEVS, SLOTS), 0, GROUP_TILES), jax.random.fold_in(key_of[3], 1), 0, GROUP_TILES - 1).astype(jnp.int32)
    counts = draw_counts(jax.random.fold_in(key_of[5], 71), 0)
    return dict(embedding=embedding, tile_blocks=tile_blocks, tile_row=tile_row, tile_col=tile_col, counts=counts)


def apply_operator(values_bf, tile_blocks, tile_row, tile_col, counts):
    blocks = values_bf.reshape(NODES // TILE, TILE, EMB)

    def add_tile(carry, flat_index):
        wide_pos = flat_index // (N_NARROW * SLOTS)
        narrow_pos = flat_index // SLOTS % N_NARROW
        slot = flat_index % SLOTS
        column = tile_col[wide_pos, narrow_pos, slot]
        global_col = (column // TILE_ROWS * N_NARROW + narrow_pos) * TILE_ROWS + column % TILE_ROWS
        global_row = wide_pos * N_NARROW * TILE_ROWS + tile_row[wide_pos, narrow_pos, slot]

        def compute(accum):
            product = jnp.dot(tile_blocks[wide_pos, narrow_pos, slot].astype(jnp.float32), blocks[global_col].astype(jnp.float32), preferred_element_type=jnp.float32)
            return accum.at[global_row].add(product)

        def keep(accum):
            return accum
        carry = lax.cond(slot < counts[wide_pos, narrow_pos], compute, keep, carry)
        return (carry, None)
    start = jnp.zeros((NODES // TILE, TILE, EMB), jnp.float32)
    result, unused = lax.scan(add_tile, start, jnp.arange(N_WIDE * N_NARROW * SLOTS, dtype=jnp.int32))
    return result.reshape(NODES, EMB)

def reference(embedding, tile_blocks, tile_row, tile_col, counts):
    emb_bf = embedding.astype(jnp.bfloat16)
    first_order = apply_operator(emb_bf, tile_blocks, tile_row, tile_col, counts)
    first_bf = first_order.astype(jnp.bfloat16)
    second = 2.0 * apply_operator(first_bf, tile_blocks, tile_row, tile_col, counts) - embedding
    spectral = 1.2661 * embedding - 1.1303 * first_order + 0.2715 * second
    gram_matrix = lax.dot_general(spectral, spectral, (((0,), (0,)), ((), ())), precision=lax.Precision.HIGHEST)
    lower_factor = jnp.linalg.cholesky(gram_matrix)
    solved = jax.scipy.linalg.solve_triangular(lower_factor, spectral.T, lower=True)
    return solved.T * jnp.sqrt(jnp.float32(NODES))
```

```python
import functools

import jax
import jax.numpy as jnp
from jax import lax
from jax.experimental import pallas as pl
from jax.experimental.pallas import tpu as pltpu
from jax.sharding import PartitionSpec as P

MESH = pl.DeviceIdType.MESH
BF = jnp.bfloat16
F32 = jnp.float32


def spread_kernel(
    n_wide, n_narrow, emb_ref, tiles_ref, row_ref, col_ref, count_ref, spec_ref, gram_ref,
    tiles, gath_a, gath_b, acc, first, pair_in, far_out, far_in, gram_part, gram_in, gram_sum, gram_wide, gram_all,
    tile_sem, line_send, line_recv, side_send, side_recv, pair_send, pair_recv, far_send, far_recv,
    g1_send, g1_recv, g2_send, g2_recv, g3_send, g3_recv,
):
    slots = tiles.shape[0]
    gath = (gath_a, gath_b)
    minor = 2 if n_wide % 2 == 0 else 1
    major = n_wide // minor
    halves = n_narrow // 2
    w, n = lax.axis_index("wide"), lax.axis_index("narrow")
    a, b = w // minor, w % minor
    p, c = n // 2, n % 2

    def remote(src, dst, send, recv, to):
        return pltpu.make_async_remote_copy(
            src_ref=src, dst_ref=dst, send_sem=send, recv_sem=recv, device_id=to, device_id_type=MESH
        )

    def each(lo, hi, body):
        lax.fori_loop(lo, hi, lambda k, z: (body(k), z)[1], 0)

    def tile_copy(s):
        return pltpu.make_async_copy(tiles_ref.at[s], tiles.at[s], tile_sem.at[s])

    barrier = pltpu.get_barrier_semaphore()
    each(1, n_wide, lambda k: pl.semaphore_signal(
        barrier, inc=1, device_id=((w + k) % n_wide, n), device_id_type=MESH))
    each(1, n_narrow, lambda k: pl.semaphore_signal(
        barrier, inc=1, device_id=(w, (n + k) % n_narrow), device_id_type=MESH))
    each(0, slots, lambda s: tile_copy(s).start())
    gath_a[w] = emb_ref[...].astype(BF)
    pl.semaphore_wait(barrier, n_wide - 1 + n_narrow - 1)

    def gather(t):
        def line(k):
            return remote(gath[t].at[w], gath[t].at[w], line_send.at[t, k], line_recv.at[t, k],
                          ((a + k) % major * minor + b, n))

        def side(k):
            own = (a + major - k) % major * minor + b
            return remote(gath[t].at[own], gath[t].at[own], side_send.at[t, k], side_recv.at[t, k],
                          (a * minor + 1 - b, n))

        each(1, major, lambda k: line(k).start())
        if minor == 2:
            side(0).start()

        def relay(k):
            line(k).wait_recv()
            if minor == 2:
                side(k).start()

        each(1, major, relay)
        if minor == 2:
            each(0, major, lambda k: side(k).wait_recv())

        def finish():
            each(1, major, lambda k: line(k).wait_send())
            if minor == 2:
                each(0, major, lambda k: side(k).wait_send())

        return finish

    def product(t):
        acc[...] = jnp.zeros_like(acc)
        group = 2 if slots % 2 == 0 else 1

        def step(i, z):
            prods = []
            for u in range(group):
                s = i * group + u
                value = jnp.dot(tiles[s], gath[t][col_ref[s]], preferred_element_type=F32)
                prods.append((value, jnp.where(s < count_ref[0], row_ref[s], -1)))
            for q in range(n_narrow):
                total = acc[q]
                for value, row in prods:
                    total = total + jnp.where(row == q, value, 0.0)
                acc[q] = total
            return z

        lax.fori_loop(0, slots // group, step, 0)

    def reduce(t):
        def pair(h):
            return remote(acc.at[2 * h + 1 - c], pair_in.at[t, h], pair_send.at[t, h], pair_recv.at[t, h],
                          (w, 2 * p + 1 - c))

        def far(k):
            return remote(far_out.at[t, k], far_in.at[t, k], far_send.at[t, k], far_recv.at[t, k],
                          (w, (p + k) % halves * 2 + c))

        for k in range(1, halves + 1):
            pair((p + k) % halves).start()
        for k in range(1, halves):
            h = (p + k) % halves
            pair(h).wait_recv()
            far_out[t, k] = (acc[2 * h + c] + pair_in[t, h]).astype(BF)
            far(k).start()
        pair(p).wait_recv()
        total = acc[n] + pair_in[t, p]
        for k in range(1, halves):
            far(k).wait_recv()
            total = total + far_in[t, k].astype(F32)
        for k in range(1, halves):
            far(k).wait_send()
        each(0, halves, lambda h: pair(h).wait_send())
        return total

    done = gather(0)
    each(0, slots, lambda s: tile_copy(s).wait())
    product(0)
    done()
    total = reduce(0)
    first[...] = total
    gath_b[w] = total.astype(BF)
    done = gather(1)
    product(1)
    done()
    second = 2.0 * reduce(1) - emb_ref[...]
    spectral = 1.2661 * emb_ref[...] - 1.1303 * first[...] + 0.2715 * second
    spec_ref[...] = spectral
    gram = lax.dot_general(spectral, spectral, (((0,), (0,)), ((), ())),
                           precision=lax.Precision.HIGHEST, preferred_element_type=F32)
    gram_part[...] = gram.reshape(gram_part.shape)

    def g1(k):
        return remote(gram_part.at[(n + k) % n_narrow], gram_in.at[k], g1_send.at[k], g1_recv.at[k],
                      (w, (n + k) % n_narrow))

    def g2(k):
        return remote(gram_wide.at[w], gram_wide.at[w], g2_send.at[k], g2_recv.at[k],
                      ((w + k) % n_wide, n))

    def g3(k):
        return remote(gram_all.at[n], gram_all.at[n], g3_send.at[k], g3_recv.at[k],
                      (w, (n + k) % n_narrow))

    for k in range(1, n_narrow):
        g1(k).start()
    part = gram_part[n]
    for k in range(1, n_narrow):
        g1(k).wait_recv()
        part = part + gram_in[k]
    gram_wide[w] = part
    each(1, n_wide, lambda k: g2(k).start())
    each(1, n_wide, lambda k: g2(k).wait_recv())
    gram_sum[...] = jnp.zeros_like(gram_sum)

    def add(k):
        gram_sum[...] += gram_wide[k]

    each(0, n_wide, add)
    gram_all[n] = gram_sum[...]
    for k in range(1, n_narrow):
        g3(k).start()
    for k in range(1, n_narrow):
        g3(k).wait_recv()
    gram_ref[...] = gram_all[...].reshape(gram_ref.shape)
    for k in range(1, n_narrow):
        g1(k).wait_send()
        g3(k).wait_send()
    each(1, n_wide, lambda k: g2(k).wait_send())


def factor_kernel(scale, spec_ref, gram_ref, out_ref):
    size = gram_ref.shape[0]
    blocks = [gram_ref[8 * i : 8 * i + 8, :] for i in range(size // 8)]
    lane = lax.broadcasted_iota(jnp.int32, (8, size), 1)
    sub = lax.broadcasted_iota(jnp.int32, (8, size), 0)
    for j in range(size):
        at, off = j // 8, j % 8
        row = blocks[at][off : off + 1, :]
        inv = 1.0 / row[:, j : j + 1]
        ratio = jnp.where(lane[:1] == j, inv, row * inv)
        for i in range(at, size // 8):
            held = blocks[i]
            new = jnp.where(lane == j, 0.0, held) - held[:, j : j + 1] * ratio
            if i == at:
                new = jnp.where(sub > off, new, held)
            blocks[i] = new
    whole = jnp.concatenate(blocks, axis=0)
    rows = lax.broadcasted_iota(jnp.int32, (size, size), 0)
    cols = lax.broadcasted_iota(jnp.int32, (size, size), 1)
    diag = jnp.sum(jnp.where(rows == cols, whole, 0.0), axis=1, keepdims=True)
    unit = jnp.where(rows == cols, 1.0, jnp.where(rows > cols, whole, 0.0))
    inverse = unit * (lax.rsqrt(diag) * scale)
    out_ref[...] = lax.dot_general(spec_ref[...], inverse, (((1,), (1,)), ((), ())),
                                   precision=lax.Precision.HIGHEST, preferred_element_type=F32)


def local(n_wide, n_narrow, embedding, tile_blocks, tile_row, tile_col, counts):
    rows, width = embedding.shape
    slots, tile = tile_blocks.shape[2], tile_blocks.shape[3]
    halves = n_narrow // 2
    band = width // n_narrow
    dma = pltpu.SemaphoreType.DMA
    vmem = pl.BlockSpec(memory_space=pltpu.VMEM)
    smem = pl.BlockSpec(memory_space=pltpu.SMEM)
    spectral, gram = pl.pallas_call(
        functools.partial(spread_kernel, n_wide, n_narrow),
        out_shape=(jax.ShapeDtypeStruct((rows, width), F32), jax.ShapeDtypeStruct((width, width), F32)),
        in_specs=[vmem, pl.BlockSpec(memory_space=pl.ANY), smem, smem, smem],
        out_specs=(vmem, vmem),
        scratch_shapes=[
            pltpu.VMEM((slots, tile, tile), BF),
            pltpu.VMEM((n_wide, rows, width), BF),
            pltpu.VMEM((n_wide, rows, width), BF),
            pltpu.VMEM((n_narrow, rows, width), F32),
            pltpu.VMEM((rows, width), F32),
            pltpu.VMEM((2, halves, rows, width), F32),
            pltpu.VMEM((2, halves, rows, width), BF),
            pltpu.VMEM((2, halves, rows, width), BF),
            pltpu.VMEM((n_narrow, band, width), F32),
            pltpu.VMEM((n_narrow, band, width), F32),
            pltpu.VMEM((band, width), F32),
            pltpu.VMEM((n_wide, band, width), F32),
            pltpu.VMEM((n_narrow, band, width), F32),
            dma((slots,)),
            dma((2, n_wide)), dma((2, n_wide)), dma((2, n_wide)), dma((2, n_wide)),
            dma((2, halves)), dma((2, halves)), dma((2, halves)), dma((2, halves)),
            dma((n_narrow,)), dma((n_narrow,)), dma((n_wide,)), dma((n_wide,)), dma((n_narrow,)), dma((n_narrow,)),
        ],
        compiler_params=pltpu.CompilerParams(
            collective_id=0, has_side_effects=True, vmem_limit_bytes=56 * 2**20
        ),
    )(embedding, tile_blocks[0, 0], tile_row[0, 0], tile_col[0, 0], counts[0])
    nodes = rows * n_wide * n_narrow
    return pl.pallas_call(
        functools.partial(factor_kernel, float(nodes) ** 0.5),
        out_shape=jax.ShapeDtypeStruct((rows, width), F32),
        in_specs=[vmem, vmem],
        out_specs=vmem,
    )(spectral, gram)


def solution(mesh):
    placed = (
        P(("wide", "narrow"), None),
        P("wide", "narrow", None, None, None),
        P("wide", "narrow", None),
        P("wide", "narrow", None),
        P("wide", "narrow"),
    )
    return jax.shard_map(
        functools.partial(local, mesh.shape["wide"], mesh.shape["narrow"]),
        mesh=mesh, in_specs=placed, out_specs=P(("wide", "narrow"), None), check_vma=False,
    )
```

```python
import functools

import jax
import jax.numpy as jnp
from jax import lax
from jax.experimental import pallas as pl
from jax.experimental.pallas import tpu as pltpu
from jax.sharding import PartitionSpec as P

MESH = pl.DeviceIdType.MESH
BF = jnp.bfloat16
F32 = jnp.float32
PIECES = 2


def spread_kernel(
    n_wide, n_narrow, emb_ref, tiles_ref, row_ref, col_ref, count_ref, spec_ref, gram_ref,
    tiles, gath_a, gath_b, acc, first, pair_in, far_out, far_in, gram_part, gram_in, gram_sum, gram_wide, gram_all,
    tile_sem, line_send, back_send, line_recv, side_send, side_recv, pair_send, pair_recv, far_send, far_recv,
    g1_send, g1_recv, g2_send, g2_recv, g3_send, g3_recv,
):
    slots = tiles.shape[0]
    gath = (gath_a, gath_b)
    minor = 2 if n_wide % 2 == 0 else 1
    major = n_wide // minor
    halves = n_narrow // 2
    w, n = lax.axis_index("wide"), lax.axis_index("narrow")
    a, b = w // minor, w % minor
    p, c = n // 2, n % 2

    def remote(src, dst, send, recv, to):
        return pltpu.make_async_remote_copy(
            src_ref=src, dst_ref=dst, send_sem=send, recv_sem=recv, device_id=to, device_id_type=MESH
        )

    def each(lo, hi, body):
        lax.fori_loop(lo, hi, lambda k, z: (body(k), z)[1], 0)

    def tile_copy(s):
        return pltpu.make_async_copy(tiles_ref.at[s], tiles.at[s], tile_sem.at[s])

    barrier = pltpu.get_barrier_semaphore()
    each(1, n_wide, lambda k: pl.semaphore_signal(
        barrier, inc=1, device_id=((w + k) % n_wide, n), device_id_type=MESH))
    each(1, n_narrow, lambda k: pl.semaphore_signal(
        barrier, inc=1, device_id=(w, (n + k) % n_narrow), device_id_type=MESH))
    each(0, slots, lambda s: tile_copy(s).start())
    gath_a[w] = emb_ref[...].astype(BF)
    pl.semaphore_wait(barrier, n_wide - 1 + n_narrow - 1)

    up, down = a + 1, a - 1
    rows = emb_ref.shape[0]
    piece = rows // PIECES

    def gather(t):
        def block(owner, h):
            return gath[t].at[owner * minor + b, pl.ds(pl.multiple_of(h * piece, piece), piece)]

        def hop(owner, h):
            here = block(owner, h)
            return remote(here, here, line_send.at[t, h, owner], line_recv.at[t, h, owner], (up * minor + b, n))

        def hop_down(owner, h):
            here = block(owner, h)
            return remote(here, here, back_send.at[t, h, owner], line_recv.at[t, h, owner], (down * minor + b, n))

        def side(owner, h):
            here = block(owner, h)
            return remote(here, here, side_send.at[t, h, owner], side_recv.at[t, h, owner], (a * minor + 1 - b, n))

        def when(cond, fn):
            pl.when(cond)(fn)

        def start(h):
            when(up < major, lambda: hop(a, h).start())
            when(down >= 0, lambda: hop_down(a, h).start())
            if minor == 2:
                side(a, h).start()

        def relay(i):
            k, h = i // PIECES + 1, i % PIECES
            lower, upper = a - k, a + k

            def from_below():
                hop(lower, h).wait_recv()
                when(up < major, lambda: hop(lower, h).start())
                if minor == 2:
                    side(lower, h).start()

            def from_above():
                hop(upper, h).wait_recv()
                when(down >= 0, lambda: hop_down(upper, h).start())
                if minor == 2:
                    side(upper, h).start()

            when(lower >= 0, from_below)
            when(upper < major, from_above)

        def relays():
            each(0, (major - 1) * PIECES, relay)
            if minor == 2:
                each(0, major * PIECES, lambda i: side(i // PIECES, i % PIECES).wait_recv())

        def finish():
            def sent(i):
                owner, h = i // PIECES, i % PIECES
                when((owner <= a) & (up < major), lambda: hop(owner, h).wait_send())
                when((owner >= a) & (down >= 0), lambda: hop_down(owner, h).wait_send())
                if minor == 2:
                    side(owner, h).wait_send()

            each(0, major * PIECES, sent)

        return start, relays, finish

    def product(t):
        acc[...] = jnp.zeros_like(acc)
        group = 2 if slots % 2 == 0 else 1

        def step(i, z):
            prods = []
            for u in range(group):
                s = i * group + u
                value = jnp.dot(tiles[s], gath[t][col_ref[s]], preferred_element_type=F32)
                prods.append((value, jnp.where(s < count_ref[0], row_ref[s], -1)))
            for q in range(n_narrow):
                total = acc[q]
                for value, row in prods:
                    total = total + jnp.where(row == q, value, 0.0)
                acc[q] = total
            return z

        lax.fori_loop(0, slots // group, step, 0)

    def reduce(t):
        def pair(h):
            return remote(acc.at[2 * h + 1 - c], pair_in.at[t, h], pair_send.at[t, h], pair_recv.at[t, h],
                          (w, 2 * p + 1 - c))

        def far(k):
            return remote(far_out.at[t, k], far_in.at[t, k], far_send.at[t, k], far_recv.at[t, k],
                          (w, (p + k) % halves * 2 + c))

        for k in range(1, halves + 1):
            pair((p + k) % halves).start()
        for k in range(1, halves):
            h = (p + k) % halves
            pair(h).wait_recv()
            far_out[t, k] = (acc[2 * h + c] + pair_in[t, h]).astype(BF)
            far(k).start()
        pair(p).wait_recv()
        total = acc[n] + pair_in[t, p]
        for k in range(1, halves):
            far(k).wait_recv()
            total = total + far_in[t, k].astype(F32)
        for k in range(1, halves):
            far(k).wait_send()
        each(0, halves, lambda h: pair(h).wait_send())
        return total

    start, relays, done = gather(0)
    for h in range(PIECES):
        start(h)
    relays()
    each(0, slots, lambda s: tile_copy(s).wait())
    product(0)
    done()
    total = reduce(0)
    first[...] = total
    gath_b[w] = total.astype(BF)
    start, relays, done = gather(1)
    for h in range(PIECES):
        start(h)
    relays()
    product(1)
    done()
    second = 2.0 * reduce(1) - emb_ref[...]
    spectral = 1.2661 * emb_ref[...] - 1.1303 * first[...] + 0.2715 * second
    spec_ref[...] = spectral
    gram = lax.dot_general(spectral, spectral, (((0,), (0,)), ((), ())),
                           precision=lax.Precision.HIGHEST, preferred_element_type=F32)
    gram_part[...] = gram.reshape(gram_part.shape)

    def g1(k):
        return remote(gram_part.at[(n + k) % n_narrow], gram_in.at[k], g1_send.at[k], g1_recv.at[k],
                      (w, (n + k) % n_narrow))

    def g2(k):
        return remote(gram_wide.at[w], gram_wide.at[w], g2_send.at[k], g2_recv.at[k],
                      ((w + k) % n_wide, n))

    def g3(k):
        return remote(gram_all.at[n], gram_all.at[n], g3_send.at[k], g3_recv.at[k],
                      (w, (n + k) % n_narrow))

    for k in range(1, n_narrow):
        g1(k).start()
    part = gram_part[n]
    for k in range(1, n_narrow):
        g1(k).wait_recv()
        part = part + gram_in[k]
    gram_wide[w] = part
    each(1, n_wide, lambda k: g2(k).start())
    each(1, n_wide, lambda k: g2(k).wait_recv())
    gram_sum[...] = jnp.zeros_like(gram_sum)

    def add(k):
        gram_sum[...] += gram_wide[k]

    each(0, n_wide, add)
    gram_all[n] = gram_sum[...]
    for k in range(1, n_narrow):
        g3(k).start()
    for k in range(1, n_narrow):
        g3(k).wait_recv()
    gram_ref[...] = gram_all[...].reshape(gram_ref.shape)
    for k in range(1, n_narrow):
        g1(k).wait_send()
        g3(k).wait_send()
    each(1, n_wide, lambda k: g2(k).wait_send())


def factor_kernel(scale, spec_ref, gram_ref, out_ref):
    size = gram_ref.shape[0]
    blocks = [gram_ref[8 * i : 8 * i + 8, :] for i in range(size // 8)]
    lane = lax.broadcasted_iota(jnp.int32, (8, size), 1)
    sub = lax.broadcasted_iota(jnp.int32, (8, size), 0)
    for at in range(size // 8):
        held = blocks[at]
        splat = [jnp.broadcast_to(held[:, 8 * at + k : 8 * at + k + 1], (8, size)) for k in range(8)]
        kept = []
        for k in range(8):
            row = held[k : k + 1, :]
            kept.append(row)
            inv = 1.0 / splat[k][k : k + 1, :]
            here = lane == 8 * at + k
            ratio = jnp.where(here[:1], inv, row * inv)
            held = jnp.where(sub == k, ratio, jnp.where(here, 0.0, held) - splat[k] * ratio)
            for m in range(k + 1, 8):
                share = splat[m][k : k + 1, :] * inv
                splat[m] = jnp.where(sub == k, share, splat[m] - splat[k] * share)
        inside = (lane >= 8 * at) & (lane < 8 * at + 8)
        blocks[at] = jnp.concatenate(kept, axis=0)
        for i in range(at + 1, size // 8):
            old = blocks[i]
            terms = [old[:, 8 * at + k : 8 * at + k + 1] * held[k : k + 1, :] for k in range(8)]
            while len(terms) > 1:
                terms = [x + y for x, y in zip(terms[::2], terms[1::2])]
            blocks[i] = jnp.where(inside, 0.0, old) - terms[0]
    whole = jnp.concatenate(blocks, axis=0)
    rows = lax.broadcasted_iota(jnp.int32, (size, size), 0)
    cols = lax.broadcasted_iota(jnp.int32, (size, size), 1)
    diag = jnp.sum(jnp.where(rows == cols, whole, 0.0), axis=1, keepdims=True)
    unit = jnp.where(rows == cols, 1.0, jnp.where(rows > cols, whole, 0.0))
    inverse = unit * (lax.rsqrt(diag) * scale)
    out_ref[...] = lax.dot_general(spec_ref[...], inverse, (((1,), (1,)), ((), ())),
                                   precision=lax.Precision.HIGHEST, preferred_element_type=F32)


def local(n_wide, n_narrow, embedding, tile_blocks, tile_row, tile_col, counts):
    rows, width = embedding.shape
    slots, tile = tile_blocks.shape[2], tile_blocks.shape[3]
    halves = n_narrow // 2
    band = width // n_narrow
    dma = pltpu.SemaphoreType.DMA
    vmem = pl.BlockSpec(memory_space=pltpu.VMEM)
    smem = pl.BlockSpec(memory_space=pltpu.SMEM)
    spectral, gram = pl.pallas_call(
        functools.partial(spread_kernel, n_wide, n_narrow),
        out_shape=(jax.ShapeDtypeStruct((rows, width), F32), jax.ShapeDtypeStruct((width, width), F32)),
        in_specs=[vmem, pl.BlockSpec(memory_space=pl.ANY), smem, smem, smem],
        out_specs=(vmem, vmem),
        scratch_shapes=[
            pltpu.VMEM((slots, tile, tile), BF),
            pltpu.VMEM((n_wide, rows, width), BF),
            pltpu.VMEM((n_wide, rows, width), BF),
            pltpu.VMEM((n_narrow, rows, width), F32),
            pltpu.VMEM((rows, width), F32),
            pltpu.VMEM((2, halves, rows, width), F32),
            pltpu.VMEM((2, halves, rows, width), BF),
            pltpu.VMEM((2, halves, rows, width), BF),
            pltpu.VMEM((n_narrow, band, width), F32),
            pltpu.VMEM((n_narrow, band, width), F32),
            pltpu.VMEM((band, width), F32),
            pltpu.VMEM((n_wide, band, width), F32),
            pltpu.VMEM((n_narrow, band, width), F32),
            dma((slots,)),
            *[dma((2, PIECES, n_wide))] * 5,
            dma((2, halves)), dma((2, halves)), dma((2, halves)), dma((2, halves)),
            dma((n_narrow,)), dma((n_narrow,)), dma((n_wide,)), dma((n_wide,)), dma((n_narrow,)), dma((n_narrow,)),
        ],
        compiler_params=pltpu.CompilerParams(
            collective_id=0, has_side_effects=True, vmem_limit_bytes=56 * 2**20
        ),
    )(embedding, tile_blocks[0, 0], tile_row[0, 0], tile_col[0, 0], counts[0])
    nodes = rows * n_wide * n_narrow
    return pl.pallas_call(
        functools.partial(factor_kernel, float(nodes) ** 0.5),
        out_shape=jax.ShapeDtypeStruct((rows, width), F32),
        in_specs=[vmem, vmem],
        out_specs=vmem,
    )(spectral, gram)


def solution(mesh):
    placed = (
        P(("wide", "narrow"), None),
        P("wide", "narrow", None, None, None),
        P("wide", "narrow", None),
        P("wide", "narrow", None),
        P("wide", "narrow"),
    )
    return jax.shard_map(
        functools.partial(local, mesh.shape["wide"], mesh.shape["narrow"]),
        mesh=mesh, in_specs=placed, out_specs=P(("wide", "narrow"), None), check_vma=False,
    )
```

```python
import functools

import jax
import jax.numpy as jnp
from jax import lax
from jax.experimental import pallas as pl
from jax.experimental.pallas import tpu as pltpu
from jax.sharding import PartitionSpec as P

MESH = pl.DeviceIdType.MESH
BF = jnp.bfloat16
F32 = jnp.float32
PIECES = 2


def spread_kernel(
    n_wide, n_narrow, emb_ref, tiles_ref, row_ref, col_ref, count_ref, spec_ref, gram_ref,
    tiles, gath_a, gath_b, acc, first, pair_in, far_out, far_in, gram_part, gram_in, gram_sum, gram_wide, gram_all,
    tile_sem, line_send, back_send, line_recv, side_send, side_recv, pair_send, pair_recv, far_send, far_recv,
    g1_send, g1_recv, g2_send, g2_recv, g3_send, g3_recv,
):
    slots = tiles.shape[0]
    gath = (gath_a, gath_b)
    minor = 2 if n_wide % 2 == 0 else 1
    major = n_wide // minor
    halves = n_narrow // 2
    w, n = lax.axis_index("wide"), lax.axis_index("narrow")
    a, b = w // minor, w % minor
    p, c = n // 2, n % 2

    def remote(src, dst, send, recv, to):
        return pltpu.make_async_remote_copy(
            src_ref=src, dst_ref=dst, send_sem=send, recv_sem=recv, device_id=to, device_id_type=MESH
        )

    def each(lo, hi, body):
        lax.fori_loop(lo, hi, lambda k, z: (body(k), z)[1], 0)

    def tile_copy(s):
        return pltpu.make_async_copy(tiles_ref.at[s], tiles.at[s], tile_sem.at[s])

    barrier = pltpu.get_barrier_semaphore()
    each(1, n_wide, lambda k: pl.semaphore_signal(
        barrier, inc=1, device_id=((w + k) % n_wide, n), device_id_type=MESH))
    each(1, n_narrow, lambda k: pl.semaphore_signal(
        barrier, inc=1, device_id=(w, (n + k) % n_narrow), device_id_type=MESH))
    each(0, slots, lambda s: tile_copy(s).start())
    gath_a[w] = emb_ref[...].astype(BF)
    pl.semaphore_wait(barrier, n_wide - 1 + n_narrow - 1)

    up, down = a + 1, a - 1
    rows = emb_ref.shape[0]
    piece = rows // PIECES

    def gather(t):
        def block(owner, h):
            return gath[t].at[owner * minor + b, pl.ds(pl.multiple_of(h * piece, piece), piece)]

        def hop(owner, h):
            here = block(owner, h)
            return remote(here, here, line_send.at[t, h, owner], line_recv.at[t, h, owner], (up * minor + b, n))

        def hop_down(owner, h):
            here = block(owner, h)
            return remote(here, here, back_send.at[t, h, owner], line_recv.at[t, h, owner], (down * minor + b, n))

        def side(owner, h):
            here = block(owner, h)
            return remote(here, here, side_send.at[t, h, owner], side_recv.at[t, h, owner], (a * minor + 1 - b, n))

        def when(cond, fn):
            pl.when(cond)(fn)

        def start(h):
            when(up < major, lambda: hop(a, h).start())
            when(down >= 0, lambda: hop_down(a, h).start())
            if minor == 2:
                side(a, h).start()

        def relay(i):
            k, h = i // PIECES + 1, i % PIECES
            lower, upper = a - k, a + k

            def from_below():
                hop(lower, h).wait_recv()
                when(up < major, lambda: hop(lower, h).start())
                if minor == 2:
                    side(lower, h).start()

            def from_above():
                hop(upper, h).wait_recv()
                when(down >= 0, lambda: hop_down(upper, h).start())
                if minor == 2:
                    side(upper, h).start()

            when(lower >= 0, from_below)
            when(upper < major, from_above)

        def relays():
            each(0, (major - 1) * PIECES, relay)
            if minor == 2:
                each(0, major * PIECES, lambda i: side(i // PIECES, i % PIECES).wait_recv())

        def finish():
            def sent(i):
                owner, h = i // PIECES, i % PIECES
                when((owner <= a) & (up < major), lambda: hop(owner, h).wait_send())
                when((owner >= a) & (down >= 0), lambda: hop_down(owner, h).wait_send())
                if minor == 2:
                    side(owner, h).wait_send()

            each(0, major * PIECES, sent)

        return start, relays, finish

    def part(h):
        return pl.ds(h * piece, piece)

    def product(t, h):
        group = 2 if slots % 2 == 0 else 1
        acc[:, part(h), :] = jnp.zeros((n_narrow, piece, acc.shape[2]), F32)

        def step(i, z):
            prods = []
            for u in range(group):
                s = i * group + u
                value = jnp.dot(tiles[s, part(h), :], gath[t][col_ref[s]], preferred_element_type=F32)
                prods.append((value, jnp.where(s < count_ref[0], row_ref[s], -1)))
            for q in range(n_narrow):
                total = acc[q, part(h), :]
                for value, row in prods:
                    total = total + jnp.where(row == q, value, 0.0)
                acc[q, part(h), :] = total
            return z

        lax.fori_loop(0, slots // group, step, 0)

    def reduce(t):
        def pair(g, h):
            return remote(acc.at[2 * g + 1 - c, part(h)], pair_in.at[t, g, part(h)],
                          pair_send.at[t, h, g], pair_recv.at[t, h, g], (w, 2 * p + 1 - c))

        def far(k, h):
            return remote(far_out.at[t, k, part(h)], far_in.at[t, k, part(h)],
                          far_send.at[t, h, k], far_recv.at[t, h, k], (w, (p + k) % halves * 2 + c))

        def share(h):
            for k in range(1, halves + 1):
                pair((p + k) % halves, h).start()

        def forward(h):
            for k in range(1, halves):
                g = (p + k) % halves
                pair(g, h).wait_recv()
                far_out[t, k, part(h), :] = (acc[2 * g + c, part(h), :] + pair_in[t, g, part(h), :]).astype(BF)
                far(k, h).start()

        def total(h):
            pair(p, h).wait_recv()
            value = acc[n, part(h), :] + pair_in[t, p, part(h), :]
            for k in range(1, halves):
                far(k, h).wait_recv()
                value = value + far_in[t, k, part(h), :].astype(F32)
            return value

        def finish():
            for h in range(PIECES):
                for k in range(1, halves):
                    far(k, h).wait_send()
                each(0, halves, lambda g: pair(g, h).wait_send())

        return share, forward, total, finish

    def rounds(t, use):
        share, forward, total, finish = reduce(t)
        for h in range(PIECES):
            product(t, h)
            share(h)
            if h:
                forward(h - 1)
        forward(PIECES - 1)
        for h in range(PIECES):
            use(h, total(h))
        finish()

    start, relays, done = gather(0)
    for h in range(PIECES):
        start(h)
    relays()
    each(0, slots, lambda s: tile_copy(s).wait())
    start, relays, done_b = gather(1)

    def keep(h, value):
        first[part(h), :] = value
        gath_b[w, part(h), :] = value.astype(BF)
        start(h)

    rounds(0, keep)
    done()
    relays()

    def combine(h, value):
        initial = emb_ref[part(h), :]
        second = 2.0 * value - initial
        spec_ref[part(h), :] = 1.2661 * initial - 1.1303 * first[part(h), :] + 0.2715 * second

    rounds(1, combine)
    done_b()
    spectral = spec_ref[...]
    gram = lax.dot_general(spectral, spectral, (((0,), (0,)), ((), ())),
                           precision=lax.Precision.HIGHEST, preferred_element_type=F32)
    gram_part[...] = gram.reshape(gram_part.shape)

    def g1(k):
        return remote(gram_part.at[(n + k) % n_narrow], gram_in.at[k], g1_send.at[k], g1_recv.at[k],
                      (w, (n + k) % n_narrow))

    def g2(k):
        return remote(gram_wide.at[w], gram_wide.at[w], g2_send.at[k], g2_recv.at[k],
                      ((w + k) % n_wide, n))

    def g3(k):
        return remote(gram_all.at[n], gram_all.at[n], g3_send.at[k], g3_recv.at[k],
                      (w, (n + k) % n_narrow))

    for k in range(1, n_narrow):
        g1(k).start()
    part = gram_part[n]
    for k in range(1, n_narrow):
        g1(k).wait_recv()
        part = part + gram_in[k]
    gram_wide[w] = part
    each(1, n_wide, lambda k: g2(k).start())
    each(1, n_wide, lambda k: g2(k).wait_recv())
    gram_sum[...] = jnp.zeros_like(gram_sum)

    def add(k):
        gram_sum[...] += gram_wide[k]

    each(0, n_wide, add)
    gram_all[n] = gram_sum[...]
    for k in range(1, n_narrow):
        g3(k).start()
    for k in range(1, n_narrow):
        g3(k).wait_recv()
    gram_ref[...] = gram_all[...].reshape(gram_ref.shape)
    for k in range(1, n_narrow):
        g1(k).wait_send()
        g3(k).wait_send()
    each(1, n_wide, lambda k: g2(k).wait_send())


def factor_kernel(scale, spec_ref, gram_ref, out_ref):
    size = gram_ref.shape[0]
    blocks = [gram_ref[8 * i : 8 * i + 8, :] for i in range(size // 8)]
    lane = lax.broadcasted_iota(jnp.int32, (8, size), 1)
    sub = lax.broadcasted_iota(jnp.int32, (8, size), 0)
    for at in range(size // 8):
        held = blocks[at]
        splat = [jnp.broadcast_to(held[:, 8 * at + k : 8 * at + k + 1], (8, size)) for k in range(8)]
        kept = []
        for k in range(8):
            row = held[k : k + 1, :]
            kept.append(row)
            inv = 1.0 / splat[k][k : k + 1, :]
            here = lane == 8 * at + k
            ratio = jnp.where(here[:1], inv, row * inv)
            held = jnp.where(sub == k, ratio, jnp.where(here, 0.0, held) - splat[k] * ratio)
            for m in range(k + 1, 8):
                share = splat[m][k : k + 1, :] * inv
                splat[m] = jnp.where(sub == k, share, splat[m] - splat[k] * share)
        inside = (lane >= 8 * at) & (lane < 8 * at + 8)
        blocks[at] = jnp.concatenate(kept, axis=0)
        for i in range(at + 1, size // 8):
            old = blocks[i]
            terms = [old[:, 8 * at + k : 8 * at + k + 1] * held[k : k + 1, :] for k in range(8)]
            while len(terms) > 1:
                terms = [x + y for x, y in zip(terms[::2], terms[1::2])]
            blocks[i] = jnp.where(inside, 0.0, old) - terms[0]
    whole = jnp.concatenate(blocks, axis=0)
    rows = lax.broadcasted_iota(jnp.int32, (size, size), 0)
    cols = lax.broadcasted_iota(jnp.int32, (size, size), 1)
    diag = jnp.sum(jnp.where(rows == cols, whole, 0.0), axis=1, keepdims=True)
    unit = jnp.where(rows == cols, 1.0, jnp.where(rows > cols, whole, 0.0))
    inverse = unit * (lax.rsqrt(diag) * scale)
    out_ref[...] = lax.dot_general(spec_ref[...], inverse, (((1,), (1,)), ((), ())),
                                   precision=lax.Precision.HIGHEST, preferred_element_type=F32)


def local(n_wide, n_narrow, embedding, tile_blocks, tile_row, tile_col, counts):
    rows, width = embedding.shape
    slots, tile = tile_blocks.shape[2], tile_blocks.shape[3]
    halves = n_narrow // 2
    band = width // n_narrow
    dma = pltpu.SemaphoreType.DMA
    vmem = pl.BlockSpec(memory_space=pltpu.VMEM)
    smem = pl.BlockSpec(memory_space=pltpu.SMEM)
    spectral, gram = pl.pallas_call(
        functools.partial(spread_kernel, n_wide, n_narrow),
        out_shape=(jax.ShapeDtypeStruct((rows, width), F32), jax.ShapeDtypeStruct((width, width), F32)),
        in_specs=[vmem, pl.BlockSpec(memory_space=pl.ANY), smem, smem, smem],
        out_specs=(vmem, vmem),
        scratch_shapes=[
            pltpu.VMEM((slots, tile, tile), BF),
            pltpu.VMEM((n_wide, rows, width), BF),
            pltpu.VMEM((n_wide, rows, width), BF),
            pltpu.VMEM((n_narrow, rows, width), F32),
            pltpu.VMEM((rows, width), F32),
            pltpu.VMEM((2, halves, rows, width), F32),
            pltpu.VMEM((2, halves, rows, width), BF),
            pltpu.VMEM((2, halves, rows, width), BF),
            pltpu.VMEM((n_narrow, band, width), F32),
            pltpu.VMEM((n_narrow, band, width), F32),
            pltpu.VMEM((band, width), F32),
            pltpu.VMEM((n_wide, band, width), F32),
            pltpu.VMEM((n_narrow, band, width), F32),
            dma((slots,)),
            *[dma((2, PIECES, n_wide))] * 5,
            *[dma((2, PIECES, halves))] * 4,
            dma((n_narrow,)), dma((n_narrow,)), dma((n_wide,)), dma((n_wide,)), dma((n_narrow,)), dma((n_narrow,)),
        ],
        compiler_params=pltpu.CompilerParams(
            collective_id=0, has_side_effects=True, vmem_limit_bytes=56 * 2**20
        ),
    )(embedding, tile_blocks[0, 0], tile_row[0, 0], tile_col[0, 0], counts[0])
    nodes = rows * n_wide * n_narrow
    return pl.pallas_call(
        functools.partial(factor_kernel, float(nodes) ** 0.5),
        out_shape=jax.ShapeDtypeStruct((rows, width), F32),
        in_specs=[vmem, vmem],
        out_specs=vmem,
    )(spectral, gram)


def solution(mesh):
    placed = (
        P(("wide", "narrow"), None),
        P("wide", "narrow", None, None, None),
        P("wide", "narrow", None),
        P("wide", "narrow", None),
        P("wide", "narrow"),
    )
    return jax.shard_map(
        functools.partial(local, mesh.shape["wide"], mesh.shape["narrow"]),
        mesh=mesh, in_specs=placed, out_specs=P(("wide", "narrow"), None), check_vma=False,
    )
```

```python
import functools

import jax
import jax.numpy as jnp
from jax import lax
from jax.experimental import pallas as pl
from jax.experimental.pallas import tpu as pltpu
from jax.sharding import PartitionSpec as P

MESH = pl.DeviceIdType.MESH
BF = jnp.bfloat16
F32 = jnp.float32
PIECES = 4


def spread_kernel(
    n_wide, n_narrow, emb_ref, tiles_ref, row_ref, col_ref, count_ref, spec_ref, gram_ref,
    tiles, gath_a, gath_b, acc, first, pair_in, far_out, far_in, gram_part, gram_in, gram_sum, gram_wide, gram_all,
    tile_sem, line_send, back_send, line_recv, side_send, side_recv, pair_send, pair_recv, far_send, far_recv,
    g1_send, g1_recv, g2_send, g2_recv, g3_send, g3_recv,
):
    slots = tiles.shape[0]
    gath = (gath_a, gath_b)
    minor = 2 if n_wide % 2 == 0 else 1
    major = n_wide // minor
    halves = n_narrow // 2
    w, n = lax.axis_index("wide"), lax.axis_index("narrow")
    a, b = w // minor, w % minor
    p, c = n // 2, n % 2

    def remote(src, dst, send, recv, to):
        return pltpu.make_async_remote_copy(
            src_ref=src, dst_ref=dst, send_sem=send, recv_sem=recv, device_id=to, device_id_type=MESH
        )

    def each(lo, hi, body):
        lax.fori_loop(lo, hi, lambda k, z: (body(k), z)[1], 0)

    def tile_copy(s):
        return pltpu.make_async_copy(tiles_ref.at[s], tiles.at[s], tile_sem.at[s])

    barrier = pltpu.get_barrier_semaphore()
    each(1, n_wide, lambda k: pl.semaphore_signal(
        barrier, inc=1, device_id=((w + k) % n_wide, n), device_id_type=MESH))
    each(1, n_narrow, lambda k: pl.semaphore_signal(
        barrier, inc=1, device_id=(w, (n + k) % n_narrow), device_id_type=MESH))
    each(0, slots, lambda s: tile_copy(s).start())
    gath_a[w] = emb_ref[...].astype(BF)
    pl.semaphore_wait(barrier, n_wide - 1 + n_narrow - 1)

    up, down = a + 1, a - 1
    rows = emb_ref.shape[0]
    piece = rows // PIECES

    def gather(t):
        def block(owner, h):
            return gath[t].at[owner * minor + b, pl.ds(pl.multiple_of(h * piece, piece), piece)]

        def hop(owner, h):
            here = block(owner, h)
            return remote(here, here, line_send.at[t, h, owner], line_recv.at[t, h, owner], (up * minor + b, n))

        def hop_down(owner, h):
            here = block(owner, h)
            return remote(here, here, back_send.at[t, h, owner], line_recv.at[t, h, owner], (down * minor + b, n))

        def side(owner, h):
            here = block(owner, h)
            return remote(here, here, side_send.at[t, h, owner], side_recv.at[t, h, owner], (a * minor + 1 - b, n))

        def when(cond, fn):
            pl.when(cond)(fn)

        def start(h):
            when(up < major, lambda: hop(a, h).start())
            when(down >= 0, lambda: hop_down(a, h).start())
            if minor == 2:
                side(a, h).start()

        def relay(i):
            k, h = i // PIECES + 1, i % PIECES
            lower, upper = a - k, a + k

            def from_below():
                hop(lower, h).wait_recv()
                when(up < major, lambda: hop(lower, h).start())
                if minor == 2:
                    side(lower, h).start()

            def from_above():
                hop(upper, h).wait_recv()
                when(down >= 0, lambda: hop_down(upper, h).start())
                if minor == 2:
                    side(upper, h).start()

            when(lower >= 0, from_below)
            when(upper < major, from_above)

        def relays():
            each(0, (major - 1) * PIECES, relay)
            if minor == 2:
                each(0, major * PIECES, lambda i: side(i // PIECES, i % PIECES).wait_recv())

        def finish():
            def sent(i):
                owner, h = i // PIECES, i % PIECES
                when((owner <= a) & (up < major), lambda: hop(owner, h).wait_send())
                when((owner >= a) & (down >= 0), lambda: hop_down(owner, h).wait_send())
                if minor == 2:
                    side(owner, h).wait_send()

            each(0, major * PIECES, sent)

        return start, relays, finish

    def part(h):
        return pl.ds(h * piece, piece)

    def product(t, h):
        group = max(g for g in range(1, 12) if slots % g == 0)
        acc[:, part(h), :] = jnp.zeros((n_narrow, piece, acc.shape[2]), F32)

        def step(i, z):
            prods = []
            for u in range(group):
                s = i * group + u
                value = jnp.dot(tiles[s, part(h), :], gath[t][col_ref[s]], preferred_element_type=F32)
                prods.append((value, jnp.where(s < count_ref[0], row_ref[s], -1)))
            for q in range(n_narrow):
                total = acc[q, part(h), :]
                for value, row in prods:
                    total = total + jnp.where(row == q, value, 0.0)
                acc[q, part(h), :] = total
            return z

        lax.fori_loop(0, slots // group, step, 0)

    def reduce(t):
        def pair(g, h):
            return remote(acc.at[2 * g + 1 - c, part(h)], pair_in.at[t, g, part(h)],
                          pair_send.at[t, h, g], pair_recv.at[t, h, g], (w, 2 * p + 1 - c))

        def far(k, h):
            return remote(far_out.at[t, k, part(h)], far_in.at[t, k, part(h)],
                          far_send.at[t, h, k], far_recv.at[t, h, k], (w, (p + k) % halves * 2 + c))

        def share(h):
            for k in range(1, halves + 1):
                pair((p + k) % halves, h).start()

        def forward(h):
            for k in range(1, halves):
                g = (p + k) % halves
                pair(g, h).wait_recv()
                far_out[t, k, part(h), :] = (acc[2 * g + c, part(h), :] + pair_in[t, g, part(h), :]).astype(BF)
                far(k, h).start()

        def total(h):
            pair(p, h).wait_recv()
            value = acc[n, part(h), :] + pair_in[t, p, part(h), :]
            for k in range(1, halves):
                far(k, h).wait_recv()
                value = value + far_in[t, k, part(h), :].astype(F32)
            return value

        def finish():
            for h in range(PIECES):
                for k in range(1, halves):
                    far(k, h).wait_send()
                each(0, halves, lambda g: pair(g, h).wait_send())

        return share, forward, total, finish

    def rounds(t, use):
        share, forward, total, finish = reduce(t)
        for h in range(PIECES):
            product(t, h)
            share(h)
            if h:
                forward(h - 1)
        forward(PIECES - 1)
        for h in range(PIECES):
            use(h, total(h))
        finish()

    start, relays, done = gather(0)
    for h in range(PIECES):
        start(h)
    relays()
    each(0, slots, lambda s: tile_copy(s).wait())
    start, relays, done_b = gather(1)

    def keep(h, value):
        first[part(h), :] = value
        gath_b[w, part(h), :] = value.astype(BF)
        start(h)

    rounds(0, keep)
    done()
    relays()

    def combine(h, value):
        initial = emb_ref[part(h), :]
        second = 2.0 * value - initial
        spec_ref[part(h), :] = 1.2661 * initial - 1.1303 * first[part(h), :] + 0.2715 * second

    rounds(1, combine)
    done_b()
    spectral = spec_ref[...]
    gram = lax.dot_general(spectral, spectral, (((0,), (0,)), ((), ())),
                           precision=lax.Precision.HIGHEST, preferred_element_type=F32)
    gram_part[...] = gram.reshape(gram_part.shape)

    def g1(k):
        return remote(gram_part.at[(n + k) % n_narrow], gram_in.at[k], g1_send.at[k], g1_recv.at[k],
                      (w, (n + k) % n_narrow))

    def g2(k):
        return remote(gram_wide.at[w], gram_wide.at[w], g2_send.at[k], g2_recv.at[k],
                      ((w + k) % n_wide, n))

    def g3(k):
        return remote(gram_all.at[n], gram_all.at[n], g3_send.at[k], g3_recv.at[k],
                      (w, (n + k) % n_narrow))

    for k in range(1, n_narrow):
        g1(k).start()
    part = gram_part[n]
    for k in range(1, n_narrow):
        g1(k).wait_recv()
        part = part + gram_in[k]
    gram_wide[w] = part
    each(1, n_wide, lambda k: g2(k).start())
    each(1, n_wide, lambda k: g2(k).wait_recv())
    gram_sum[...] = jnp.zeros_like(gram_sum)

    def add(k):
        gram_sum[...] += gram_wide[k]

    each(0, n_wide, add)
    gram_all[n] = gram_sum[...]
    for k in range(1, n_narrow):
        g3(k).start()
    for k in range(1, n_narrow):
        g3(k).wait_recv()
    gram_ref[...] = gram_all[...].reshape(gram_ref.shape)
    for k in range(1, n_narrow):
        g1(k).wait_send()
        g3(k).wait_send()
    each(1, n_wide, lambda k: g2(k).wait_send())


def factor_kernel(scale, spec_ref, gram_ref, out_ref):
    size = gram_ref.shape[0]
    blocks = [gram_ref[8 * i : 8 * i + 8, :] for i in range(size // 8)]
    lane = lax.broadcasted_iota(jnp.int32, (8, size), 1)
    sub = lax.broadcasted_iota(jnp.int32, (8, size), 0)
    for at in range(size // 8):
        held = blocks[at]
        splat = [jnp.broadcast_to(held[:, 8 * at + k : 8 * at + k + 1], (8, size)) for k in range(8)]
        kept = []
        for k in range(8):
            row = held[k : k + 1, :]
            kept.append(row)
            inv = 1.0 / splat[k][k : k + 1, :]
            here = lane == 8 * at + k
            ratio = jnp.where(here[:1], inv, row * inv)
            held = jnp.where(sub == k, ratio, jnp.where(here, 0.0, held) - splat[k] * ratio)
            for m in range(k + 1, 8):
                share = splat[m][k : k + 1, :] * inv
                splat[m] = jnp.where(sub == k, share, splat[m] - splat[k] * share)
        inside = (lane >= 8 * at) & (lane < 8 * at + 8)
        blocks[at] = jnp.concatenate(kept, axis=0)
        for i in range(at + 1, size // 8):
            old = blocks[i]
            terms = [old[:, 8 * at + k : 8 * at + k + 1] * held[k : k + 1, :] for k in range(8)]
            while len(terms) > 1:
                terms = [x + y for x, y in zip(terms[::2], terms[1::2])]
            blocks[i] = jnp.where(inside, 0.0, old) - terms[0]
    whole = jnp.concatenate(blocks, axis=0)
    rows = lax.broadcasted_iota(jnp.int32, (size, size), 0)
    cols = lax.broadcasted_iota(jnp.int32, (size, size), 1)
    diag = jnp.sum(jnp.where(rows == cols, whole, 0.0), axis=1, keepdims=True)
    unit = jnp.where(rows == cols, 1.0, jnp.where(rows > cols, whole, 0.0))
    inverse = unit * (lax.rsqrt(diag) * scale)
    out_ref[...] = lax.dot_general(spec_ref[...], inverse, (((1,), (1,)), ((), ())),
                                   precision=lax.Precision.HIGHEST, preferred_element_type=F32)


def local(n_wide, n_narrow, embedding, tile_blocks, tile_row, tile_col, counts):
    rows, width = embedding.shape
    slots, tile = tile_blocks.shape[2], tile_blocks.shape[3]
    halves = n_narrow // 2
    band = width // n_narrow
    dma = pltpu.SemaphoreType.DMA
    vmem = pl.BlockSpec(memory_space=pltpu.VMEM)
    smem = pl.BlockSpec(memory_space=pltpu.SMEM)
    spectral, gram = pl.pallas_call(
        functools.partial(spread_kernel, n_wide, n_narrow),
        out_shape=(jax.ShapeDtypeStruct((rows, width), F32), jax.ShapeDtypeStruct((width, width), F32)),
        in_specs=[vmem, pl.BlockSpec(memory_space=pl.ANY), smem, smem, smem],
        out_specs=(vmem, vmem),
        scratch_shapes=[
            pltpu.VMEM((slots, tile, tile), BF),
            pltpu.VMEM((n_wide, rows, width), BF),
            pltpu.VMEM((n_wide, rows, width), BF),
            pltpu.VMEM((n_narrow, rows, width), F32),
            pltpu.VMEM((rows, width), F32),
            pltpu.VMEM((2, halves, rows, width), F32),
            pltpu.VMEM((2, halves, rows, width), BF),
            pltpu.VMEM((2, halves, rows, width), BF),
            pltpu.VMEM((n_narrow, band, width), F32),
            pltpu.VMEM((n_narrow, band, width), F32),
            pltpu.VMEM((band, width), F32),
            pltpu.VMEM((n_wide, band, width), F32),
            pltpu.VMEM((n_narrow, band, width), F32),
            dma((slots,)),
            *[dma((2, PIECES, n_wide))] * 5,
            *[dma((2, PIECES, halves))] * 4,
            dma((n_narrow,)), dma((n_narrow,)), dma((n_wide,)), dma((n_wide,)), dma((n_narrow,)), dma((n_narrow,)),
        ],
        compiler_params=pltpu.CompilerParams(
            collective_id=0, has_side_effects=True, vmem_limit_bytes=56 * 2**20
        ),
    )(embedding, tile_blocks[0, 0], tile_row[0, 0], tile_col[0, 0], counts[0])
    nodes = rows * n_wide * n_narrow
    return pl.pallas_call(
        functools.partial(factor_kernel, float(nodes) ** 0.5),
        out_shape=jax.ShapeDtypeStruct((rows, width), F32),
        in_specs=[vmem, vmem],
        out_specs=vmem,
    )(spectral, gram)


def solution(mesh):
    placed = (
        P(("wide", "narrow"), None),
        P("wide", "narrow", None, None, None),
        P("wide", "narrow", None),
        P("wide", "narrow", None),
        P("wide", "narrow"),
    )
    return jax.shard_map(
        functools.partial(local, mesh.shape["wide"], mesh.shape["narrow"]),
        mesh=mesh, in_specs=placed, out_specs=P(("wide", "narrow"), None), check_vma=False,
    )
```
